256 devices in a mesh: row: 8 (over y_hi, x), col: 32 (over y_lo, z, core).
Axes of the slice: x: 4, y: 4 (y_hi: 2, y_lo: 2; y = y_hi * 2 + y_lo), z: 8, core: 2. Of those that a mesh axis runs over, the one named last changes fastest.
Arguments:
- inputs: bfloat16 [768, 8192], P('col', 'row'), may hold values from -6 to 6
- grad_out: bfloat16 [768, 8192], P('col', 'row'), may hold values from -1.5 to 1.5
- gate_weight: bfloat16 [8192, 28672], P('row', 'col'), may hold values from -0.0625 to 0.0625
- up_weight: bfloat16 [8192, 28672], P('row', 'col'), may hold values from -0.0625 to 0.0625
- down_weight: bfloat16 [28672, 8192], P('col', 'row'), may hold values from -0.03125 to 0.03125
Outputs:
- input_grad: bfloat16 [768, 8192], P('col', 'row')
- gate_grad: bfloat16 [8192, 28672], P('row', 'col')
- up_grad: bfloat16 [8192, 28672], P('row', 'col')
- down_grad: bfloat16 [28672, 8192], P('col', 'row')
The draws below stay inside these ranges and needn't reach their ends.
All inputs are finite; a program needn't handle non-finite values.
Results may differ from the reference program's by a relative error of at most 0.0049.
Values may be sent and summed in bfloat16 or wider, within the bound.
No kernel may reach another device: no remote copies, remote signals or barrier semaphores. Data moves between devices by JAX's collectives and lax.ppermute only.
A program may use at most 128 MiB of HBM per device.

```python
import jax
import jax.numpy as jnp
from jax import lax

D = 8192
FF = 28672
TOKENS = 768


def steps_of(stream_key, extent, cuts, smallest, largest):
    def one(position, blocks):
        steps = jax.random.uniform(jax.random.fold_in(jax.random.fold_in(stream_key, 6), position), (blocks,), jnp.float32, smallest / len(cuts), largest / len(cuts))
        return jnp.repeat(jnp.exp(steps), extent[position] // blocks).reshape((-1,) + (1,) * (len(extent) - position - 1))

    gain = one(*cuts[0])
    for cut in cuts[1:]:
        gain = gain * one(*cut)
    return gain


def noise(own_key, dims, deviation, limit, cuts=(), kind=jnp.bfloat16):
    drawn = deviation * jax.random.normal(own_key, dims, jnp.float32)
    if cuts:
        drawn = drawn * steps_of(own_key, dims, cuts, -0.22, 0.18)
    return jnp.clip(drawn, -limit, limit).astype(kind)


def setup_inputs(seed: int = 0) -> dict:
    key_list = jax.random.split(jax.random.key(seed), 6)
    inputs = noise(key_list[0], (TOKENS, D), 1.0, 6.0, ((0, 32), (1, 8)))
    grad_out = noise(key_list[1], (TOKENS, D), 0.25, 1.5, ((0, 32), (1, 8)))
    gate_weight = noise(key_list[2], (D, FF), D ** -0.5, 0.0625, ((0, 8), (1, 32)))
    up_weight = noise(key_list[3], (D, FF), D ** -0.5, 0.0625, ((0, 8), (1, 32)))
    down_weight = noise(key_list[4], (FF, D), FF ** -0.5, 0.03125, ((0, 32), (1, 8)))
    return dict(inputs=inputs, grad_out=grad_out, gate_weight=gate_weight, up_weight=up_weight, down_weight=down_weight)


def reference(inputs, grad_out, gate_weight, up_weight, down_weight):
    contract_last = (((1,), (1,)), ((), ()))
    contract_first = (((0,), (0,)), ((), ()))
    gate = jnp.dot(inputs, gate_weight, preferred_element_type=jnp.float32)
    up = jnp.dot(inputs, up_weight, preferred_element_type=jnp.float32)
    grad_hidden = lax.dot_general(grad_out, down_weight, contract_last, preferred_element_type=jnp.float32)
    sigmoid_gate = jax.nn.sigmoid(gate)
    act = gate * sigmoid_gate
    hidden = (act * up).astype(jnp.bfloat16)
    grad_gate = (grad_hidden * up * sigmoid_gate * (1.0 + gate * (1.0 - sigmoid_gate))).astype(jnp.bfloat16)
    grad_up = (grad_hidden * act).astype(jnp.bfloat16)
    input_grad = lax.dot_general(grad_gate, gate_weight, contract_last, preferred_element_type=jnp.float32)
    input_grad = input_grad + lax.dot_general(grad_up, up_weight, contract_last, preferred_element_type=jnp.float32)
    gate_grad = lax.dot_general(inputs, grad_gate, contract_first, preferred_element_type=jnp.float32)
    up_grad = lax.dot_general(inputs, grad_up, contract_first, preferred_element_type=jnp.float32)
    down_grad = lax.dot_general(hidden, grad_out, contract_first, preferred_element_type=jnp.float32)
    return (input_grad.astype(jnp.bfloat16), gate_grad.astype(jnp.bfloat16),
            up_grad.astype(jnp.bfloat16), down_grad.astype(jnp.bfloat16))
```

```python
import jax
import jax.numpy as jnp
from jax import lax
from jax.sharding import PartitionSpec as P

BF, F32 = jnp.bfloat16, jnp.float32
YH, X, YL, Z, CORE = 2, 4, 2, 8, 2
LAST = (((1,), (1,)), ((), ()))
FIRST = (((0,), (0,)), ((), ()))


def from_x(block, k):
    pairs = [(h * X + (x + k) % X, h * X + x) for h in range(YH) for x in range(X)]
    return lax.ppermute(block, "row", pairs)


def from_yh(block):
    return lax.ppermute(block, "row", [(i, (i + X) % (X * YH)) for i in range(X * YH)])


def from_col(block, source):
    pairs = []
    for yl in range(YL):
        for z in range(Z):
            for core in range(CORE):
                a, b, c = source(yl, z, core)
                pairs.append(((a * Z + b % Z) * CORE + c, (yl * Z + z) * CORE + core))
    return lax.ppermute(block, "col", pairs)


def from_z(block, k):
    return from_col(block, lambda yl, z, core: (yl, z + k, core))


def from_yl(block):
    return from_col(block, lambda yl, z, core: (1 - yl, z, core))


def from_core(block):
    return from_col(block, lambda yl, z, core: (yl, z, 1 - core))


def dot(a, b):
    return jnp.dot(a, b, preferred_element_type=F32)


def dot_last(a, b):
    return lax.dot_general(a, b, LAST, preferred_element_type=F32)


def dot_first(a, b):
    return lax.dot_general(a, b, FIRST, preferred_element_type=F32)


def swiglu_back(gate, up, grad_hidden):
    sigmoid_gate = jax.nn.sigmoid(gate)
    act = gate * sigmoid_gate
    hidden = (act * up).astype(BF)
    grad_gate = (grad_hidden * up * sigmoid_gate * (1.0 + gate * (1.0 - sigmoid_gate))).astype(BF)
    grad_up = (grad_hidden * act).astype(BF)
    return jnp.stack([hidden, grad_gate, grad_up])


def rolled(tokens, yh, x):
    tokens = lax.dynamic_slice_in_dim(jnp.concatenate([tokens, tokens], 1), x, X, 1)
    return lax.dynamic_slice_in_dim(jnp.concatenate([tokens, tokens], 0), yh, YH, 0)


def on_device(inputs, grad_out, gate_weight, up_weight, down_weight):
    row = lax.axis_index("row")
    yh, x = row // X, row % X
    t, d = inputs.shape
    f = gate_weight.shape[1]
    pair = 2 * t

    own = jnp.stack([inputs, grad_out])
    by_z = jnp.stack([own] + [from_z(own, k) for k in range(1, Z)], 1)
    by_z_b = from_yl(by_z)
    a_tokens = jnp.stack([by_z, from_core(by_z)], 1).reshape(2, CORE, X, pair, d)
    b_tokens = jnp.stack([by_z_b, from_core(by_z_b)], 1).reshape(2, CORE, X, pair, d)
    xa, ga = (rolled(a_tokens[i], yh, x).transpose(1, 0, 2, 3).reshape(X * YH * pair, d) for i in (0, 1))
    xb, gb = (rolled(b_tokens[i], yh, x).reshape(X * YH * pair, d) for i in (0, 1))

    def partials(tokens, grads):
        return (dot(tokens, gate_weight), dot(tokens, up_weight), dot_last(grads, down_weight))

    cut = YH * pair
    away = [p.astype(BF).reshape(X - 1, cut, f) for p in partials(xa[cut:], ga[cut:])]
    total = jnp.stack(partials(xa[:cut], ga[:cut]))
    for k in range(1, X):
        total = total + from_x(jnp.stack([p[k - 1] for p in away]), X - k).astype(F32)
    total = total.reshape(3, YH, pair, f)
    total = total[:, 0] + from_yh(total[:, 1].astype(BF)).astype(F32)
    a_rows = swiglu_back(*total)

    cut = X * pair
    away = jnp.stack([p.astype(BF) for p in partials(xb[cut:], gb[cut:])])
    total = jnp.stack(partials(xb[:cut], gb[:cut])) + from_yh(away).astype(F32)
    total = total.reshape(3, X, pair, f)
    away = total[:, 1:].astype(BF)
    total = total[:, 0]
    for k in range(1, X):
        total = total + from_x(away[:, k - 1], X - k).astype(F32)
    b_rows = swiglu_back(*total)

    a_half = jnp.stack([a_rows, from_yh(a_rows)], 1)
    a_all = jnp.stack([a_half] + [from_x(a_half, k) for k in range(1, X)], 1).reshape(3, -1, f)
    b_half = jnp.stack([b_rows] + [from_x(b_rows, k) for k in range(1, X)], 1)
    b_all = jnp.stack([b_half, from_yh(b_half)], 1).reshape(3, -1, f)

    def input_terms(rows):
        return dot_last(rows[1], gate_weight) + dot_last(rows[2], up_weight)

    def over_core(terms, axis):
        mine = lax.dynamic_index_in_dim(terms, yh, axis, keepdims=False)
        other = lax.dynamic_index_in_dim(terms, 1 - yh, axis, keepdims=False)
        return mine + from_core(other)

    a_terms = over_core(input_terms(a_all).reshape(X, YH, pair, d), 1)
    b_terms = over_core(input_terms(b_all).reshape(YH, X, pair, d), 0)
    terms = a_terms + from_yl(b_terms.astype(BF)).astype(F32)
    terms = terms.reshape(Z, t, d)
    terms = lax.dynamic_slice_in_dim(jnp.concatenate([terms, terms], 0), Z - 2 * x, Z, 0)
    away = terms[1:].astype(BF)
    input_grad = terms[0]
    for k in range(1, Z):
        input_grad = input_grad + from_z(away[k - 1], Z - k).astype(F32)

    tokens_all = jnp.concatenate([xa, xb])
    grads_all = jnp.concatenate([ga, gb])
    hidden, grad_gate, grad_up = (jnp.concatenate([a_all[i], b_all[i]]) for i in range(3))
    gate_grad = dot_first(tokens_all, grad_gate)
    up_grad = dot_first(tokens_all, grad_up)
    down_grad = dot_first(hidden, grads_all)
    return (input_grad.astype(BF), gate_grad.astype(BF), up_grad.astype(BF), down_grad.astype(BF))


def solution(mesh):
    in_specs = (P("col", "row"), P("col", "row"), P("row", "col"), P("row", "col"), P("col", "row"))
    out_specs = (P("col", "row"), P("row", "col"), P("row", "col"), P("col", "row"))
    return jax.shard_map(
        on_device, mesh=mesh, in_specs=in_specs, out_specs=out_specs, check_vma=False
    )
```

```python
import jax
import jax.numpy as jnp
from jax import lax
from jax.experimental import pallas as pl
from jax.experimental.pallas import tpu as pltpu
from jax.sharding import PartitionSpec as P

BF, F32 = jnp.bfloat16, jnp.float32
YH, X, YL, Z, CORE = 2, 4, 2, 8, 2
LAST = (((1,), (1,)), ((), ()))
FIRST = (((0,), (0,)), ((), ()))


def from_x(block, k):
    blocks = [(h * X + (x + k) % X, h * X + x) for h in range(YH) for x in range(X)]
    return lax.ppermute(block, "row", blocks)


def from_yh(block):
    return lax.ppermute(block, "row", [(i, (i + X) % (X * YH)) for i in range(X * YH)])


def from_col(block, source):
    blocks = []
    for yl in range(YL):
        for z in range(Z):
            for core in range(CORE):
                a, b, c = source(yl, z, core)
                blocks.append(((a * Z + b % Z) * CORE + c, (yl * Z + z) * CORE + core))
    return lax.ppermute(block, "col", blocks)


def from_z(block, k):
    return from_col(block, lambda yl, z, core: (yl, z + k, core))


def from_yl(block):
    return from_col(block, lambda yl, z, core: (1 - yl, z, core))


def from_core(block):
    return from_col(block, lambda yl, z, core: (yl, z, 1 - core))


def dot(a, b):
    return jnp.dot(a, b, preferred_element_type=F32)


def dot_last(a, b):
    return lax.dot_general(a, b, LAST, preferred_element_type=F32)


def dot_first(a, b):
    return lax.dot_general(a, b, FIRST, preferred_element_type=F32)


def together(*blocks):
    return lax.optimization_barrier(blocks)


def swiglu_back(gate, up, grad_hidden):
    sigmoid_gate = jax.nn.sigmoid(gate)
    act = gate * sigmoid_gate
    hidden = (act * up).astype(BF)
    grad_gate = (grad_hidden * up * sigmoid_gate * (1.0 + gate * (1.0 - sigmoid_gate))).astype(BF)
    grad_up = (grad_hidden * act).astype(BF)
    return jnp.stack([grad_gate, grad_up, hidden])


def input_terms_kernel(place, *refs):
    *row_refs, gate_ref, up_ref, mine_ref, mine_yl_ref, other_ref, other_yl_ref, rows = refs

    f = gate_ref.shape[1]

    @pl.when(pl.program_id(0) == 0)
    def _():
        start = 0
        for ref in row_refs:
            rows[start : start + ref.shape[1], :f] = ref[0]
            rows[start : start + ref.shape[1], f:] = ref[1]
            start += ref.shape[1]

    terms = dot_last(rows[...], jnp.concatenate([gate_ref[...], up_ref[...]], 1))
    t = mine_ref.shape[1]
    n = YL * t
    first = place[2 * X] == 0

    def put(at, zero, one):
        zero, one = terms[zero * n : (zero + 1) * n], terms[one * n : (one + 1) * n]
        mine, other = jnp.where(first, zero, one), jnp.where(first, one, zero)
        mine_ref[at], mine_yl_ref[at] = mine[:t], mine[t:]
        other_ref[at], other_yl_ref[at] = other[:t], other[t:]

    for k in range(X):
        put(place[k], YH * k, YH * k + 1)
        put(place[X + k], YH * X + k, YH * X + X + k)


def input_terms(place, row_blocks, gate_weight, up_weight, t):
    f, d = row_blocks[0].shape[2], gate_weight.shape[0]
    total = sum(r.shape[1] for r in row_blocks)
    wide = min(d, 256)
    whole = [pl.BlockSpec((2, r.shape[1], f), lambda i, _: (0, 0, 0)) for r in row_blocks]
    weight = pl.BlockSpec((wide, f), lambda i, _: (i, 0))
    out = pl.BlockSpec((Z, t, wide), lambda i, _: (0, 0, i))
    return pl.pallas_call(
        input_terms_kernel,
        grid_spec=pltpu.PrefetchScalarGridSpec(
            num_scalar_prefetch=1,
            grid=(d // wide,),
            in_specs=whole + [weight, weight],
            out_specs=[out] * 4,
            scratch_shapes=[pltpu.VMEM((total, 2 * f), BF)],
        ),
        out_shape=[jax.ShapeDtypeStruct((Z, t, d), F32)] * 4,
        cost_estimate=pl.CostEstimate(
            flops=4 * total * f * d, bytes_accessed=4 * total * (f + d) + 4 * d * f, transcendentals=0
        ),
        compiler_params=pltpu.CompilerParams(vmem_limit_bytes=60 << 20),
    )(place, *row_blocks, gate_weight, up_weight)


def rolled(tokens, yh, x):
    tokens = lax.dynamic_slice_in_dim(jnp.concatenate([tokens, tokens], 1), x, X, 1)
    return lax.dynamic_slice_in_dim(jnp.concatenate([tokens, tokens], 0), yh, YH, 0)


def on_device(inputs, grad_out, gate_weight, up_weight, down_weight):
    row, col = lax.axis_index("row"), lax.axis_index("col")
    yh, x, z = row // X, row % X, col // CORE % Z
    t, d = inputs.shape
    f = gate_weight.shape[1]
    block = YL * t

    own = jnp.stack([inputs, grad_out])
    own = jnp.concatenate([own, from_yl(own)], 1)
    up, down = [own], [own]
    for _ in range(Z // 2 - 1):
        up.append(from_z(up[-1], 1))
        down.append(from_z(down[-1], Z - 1))

    def tokens_of(blocks, axis):
        blocks = [(b, from_core(b)) for b in blocks]
        tokens = jnp.stack([jnp.stack([b[c] for b in blocks], 1) for c in range(CORE)], 1)
        tokens = [rolled(tokens[i], yh, x) for i in (0, 1)]
        if axis == 1:
            tokens = [b.transpose(1, 0, 2, 3) for b in tokens]
        return [b.reshape(-1, d) for b in together(*tokens)]

    def partials(both):
        p = [dot(both[0], gate_weight), dot(both[0], up_weight), dot_last(both[1], down_weight)]
        return jnp.stack(p)

    a_tokens = tokens_of([own, up[1], up[2], down[1]], 1)
    *a_tokens, up[3] = together(*a_tokens, up[3])
    up.append(from_z(up[3], 1))
    a = partials(a_tokens)
    a, up[4] = together(a, up[4])
    a = a.reshape(3, X, YH * block, f)
    b_tokens = tokens_of([up[3], up[4], down[3], down[2]], 2)
    b = partials(b_tokens).reshape(3, YH, X * block, f)
    *a_sends, b_send = together(*[a[:, k].astype(BF) for k in range(1, X)], b[:, 1].astype(BF))
    *a_parts, b_part = together(*[from_x(a_sends[k - 1], X - k) for k in range(1, X)], from_yh(b_send))

    a = a[:, 0]
    for part in a_parts:
        a = a + part.astype(F32)
    a = a.reshape(3, YH, block, f)
    b = (b[:, 0] + b_part.astype(F32)).reshape(3, X, block, f)
    *b_sends, a_send = together(*[b[:, k].astype(BF) for k in range(1, X)], a[:, 1].astype(BF))
    *b_parts, a_part = together(*[from_x(b_sends[k - 1], X - k) for k in range(1, X)], from_yh(a_send))

    a_rows = swiglu_back(*(a[:, 0] + a_part.astype(F32)))
    b = b[:, 0]
    for part in b_parts:
        b = b + part.astype(F32)
    a_rows, b_rows = together(a_rows, swiglu_back(*b))
    *b_parts, a_part = together(*[from_x(b_rows, k) for k in range(1, X)], from_yh(a_rows))

    a_half = jnp.stack([a_rows, a_part], 1).reshape(3, YH * block, f)
    b_half = jnp.stack([b_rows] + b_parts, 1).reshape(3, X * block, f)
    a_half, b_half = together(a_half, b_half)
    *a_parts, b_part = together(*[from_x(a_half, k) for k in range(1, X)], from_yh(b_half))
    order = (x + jnp.arange(X)) % X
    place = jnp.concatenate([(z + (order + 1) % X - 1) % Z, (z + 3 + order) % Z, yh[None]]).astype(jnp.int32)
    row_blocks = [a_half] + a_parts + [b_half, b_part]
    mine, mine_yl, other, other_yl = input_terms(place, row_blocks, gate_weight, up_weight, t)
    other_yl = (mine_yl + from_core(other_yl)).astype(BF)
    other, *row_blocks, _ = together(other, *row_blocks, other_yl)
    rows = [jnp.concatenate([r[i] for r in row_blocks]) for i in range(3)]
    tokens_all, grads_all = (jnp.concatenate([a_tokens[i], b_tokens[i]]) for i in (0, 1))
    terms = mine + from_core(other)
    terms, part, *rows = together(terms, from_yl(other_yl), *rows)
    terms = terms + part.astype(F32)
    groups = [[(yl * Z + i) * CORE + c for i in range(Z)] for yl in range(YL) for c in range(CORE)]
    parts = lax.all_to_all(terms.astype(BF), "col", 0, 0, axis_index_groups=groups, tiled=True)
    parts = jnp.where((jnp.arange(Z) == z)[:, None, None], 0.0, parts.astype(F32))
    input_grad = lax.dynamic_index_in_dim(terms, z, 0, keepdims=False) + parts.sum(0)

    grad_gate, grad_up, hidden = rows
    gate_grad = dot_first(tokens_all, grad_gate)
    up_grad = dot_first(tokens_all, grad_up)
    down_grad = dot_first(hidden, grads_all)
    return (input_grad.astype(BF), gate_grad.astype(BF), up_grad.astype(BF), down_grad.astype(BF))


def solution(mesh):
    in_specs = (P("col", "row"), P("col", "row"), P("row", "col"), P("row", "col"), P("col", "row"))
    out_specs = (P("col", "row"), P("row", "col"), P("row", "col"), P("col", "row"))
    return jax.shard_map(
        on_device, mesh=mesh, in_specs=in_specs, out_specs=out_specs, check_vma=False
    )
```

```python
import jax
import jax.numpy as jnp
from jax import lax
from jax.experimental import pallas as pl
from jax.experimental.pallas import tpu as pltpu
from jax.sharding import PartitionSpec as P

BF, F32 = jnp.bfloat16, jnp.float32
YH, X, YL, Z, CORE = 2, 4, 2, 8, 2
LAST = (((1,), (1,)), ((), ()))
FIRST = (((0,), (0,)), ((), ()))


def from_x(block, k):
    blocks = [(h * X + (x + k) % X, h * X + x) for h in range(YH) for x in range(X)]
    return lax.ppermute(block, "row", blocks)


def from_yh(block):
    return lax.ppermute(block, "row", [(i, (i + X) % (X * YH)) for i in range(X * YH)])


def from_col(block, source):
    blocks = []
    for yl in range(YL):
        for z in range(Z):
            for core in range(CORE):
                a, b, c = source(yl, z, core)
                blocks.append(((a * Z + b % Z) * CORE + c, (yl * Z + z) * CORE + core))
    return lax.ppermute(block, "col", blocks)


def from_z(block, k):
    return from_col(block, lambda yl, z, core: (yl, z + k, core))


def from_yl(block):
    return from_col(block, lambda yl, z, core: (1 - yl, z, core))


def from_core(block):
    return from_col(block, lambda yl, z, core: (yl, z, 1 - core))


def dot(a, b):
    return jnp.dot(a, b, preferred_element_type=F32)


def dot_last(a, b):
    return lax.dot_general(a, b, LAST, preferred_element_type=F32)


def dot_first(a, b):
    return lax.dot_general(a, b, FIRST, preferred_element_type=F32)


def together(*blocks):
    return lax.optimization_barrier(blocks)


def swiglu_back(gate, up, grad_hidden):
    sigmoid_gate = jax.nn.sigmoid(gate)
    act = gate * sigmoid_gate
    hidden = (act * up).astype(BF)
    grad_gate = (grad_hidden * up * sigmoid_gate * (1.0 + gate * (1.0 - sigmoid_gate))).astype(BF)
    grad_up = (grad_hidden * act).astype(BF)
    return jnp.stack([grad_gate, grad_up, hidden])


def input_terms_kernel(place, *refs):
    *row_refs, a_ref, b_ref, gate_ref, up_ref, mine_ref, mine_yl_ref, other_ref, other_yl_ref, rows = refs

    f = gate_ref.shape[1]

    @pl.when(pl.program_id(0) == 0)
    def _():
        start = 0
        for ref in row_refs:
            rows[start : start + ref.shape[1], :f] = ref[0]
            rows[start : start + ref.shape[1], f:] = ref[1]
            start += ref.shape[1]

    terms = dot_last(rows[...], jnp.concatenate([gate_ref[...], up_ref[...]], 1))
    t = mine_ref.shape[1]
    n = YL * t
    first = place[2 * X] == 0

    def put(at, zero, one):
        mine, other = jnp.where(first, zero, one), jnp.where(first, one, zero)
        mine_ref[at], mine_yl_ref[at] = mine[:t], mine[t:]
        other_ref[at], other_yl_ref[at] = other[:t], other[t:]

    terms = [terms[i * n : (i + 1) * n] for i in range(YH * (X - 1) + X)]
    a = [a_ref[:n], a_ref[n:]] + terms[: YH * (X - 1)]
    b = [b_ref[k * n : (k + 1) * n] for k in range(X)] + terms[YH * (X - 1) :]
    for k in range(X):
        put(place[k], a[YH * k], a[YH * k + 1])
        put(place[X + k], b[k], b[X + k])


def input_terms(place, row_blocks, a_terms, b_terms, gate_weight, up_weight, t):
    f, d = row_blocks[0].shape[2], gate_weight.shape[0]
    total = sum(r.shape[1] for r in row_blocks)
    wide = min(d, 256)
    whole = [pl.BlockSpec((2, r.shape[1], f), lambda i, _: (0, 0, 0)) for r in row_blocks]
    done = [pl.BlockSpec((b.shape[0], wide), lambda i, _: (0, i)) for b in (a_terms, b_terms)]
    weight = pl.BlockSpec((wide, f), lambda i, _: (i, 0))
    out = pl.BlockSpec((Z, t, wide), lambda i, _: (0, 0, i))
    return pl.pallas_call(
        input_terms_kernel,
        grid_spec=pltpu.PrefetchScalarGridSpec(
            num_scalar_prefetch=1,
            grid=(d // wide,),
            in_specs=whole + done + [weight, weight],
            out_specs=[out] * 4,
            scratch_shapes=[pltpu.VMEM((total, 2 * f), BF)],
        ),
        out_shape=[jax.ShapeDtypeStruct((Z, t, d), F32)] * 4,
        cost_estimate=pl.CostEstimate(
            flops=4 * total * f * d, bytes_accessed=4 * total * (f + d) + 4 * d * f, transcendentals=0
        ),
        compiler_params=pltpu.CompilerParams(vmem_limit_bytes=60 << 20),
    )(place, *row_blocks, a_terms, b_terms, gate_weight, up_weight)


def on_device(inputs, grad_out, gate_weight, up_weight, down_weight):
    row, col = lax.axis_index("row"), lax.axis_index("col")
    yh, x, z = row // X, row % X, col // CORE % Z
    t, d = inputs.shape
    f = gate_weight.shape[1]
    block = YL * t

    own = jnp.stack([inputs, grad_out])
    own = jnp.concatenate([own, from_yl(own)], 1)
    up, down = [own], [own]
    for _ in range(Z // 2 - 1):
        up.append(from_z(up[-1], 1))
        down.append(from_z(down[-1], Z - 1))

    def tokens_of(blocks, axis):
        blocks = [(b, from_core(b)) for b in blocks]
        blocks = [(jnp.where(yh == 0, *b), jnp.where(yh == 0, *b[::-1])) for b in blocks]

        def in_order(blocks):
            tokens = lax.dynamic_slice_in_dim(jnp.stack(blocks + blocks, 1), x, X, 1)
            return tokens.reshape(2, -1, d)

        if axis == 1:
            return in_order([jnp.concatenate(b, 1) for b in blocks])
        return jnp.concatenate([in_order([b[h] for b in blocks]) for h in range(YH)], 1)

    def partials(both):
        p = [dot(both[0], gate_weight), dot(both[0], up_weight), dot_last(both[1], down_weight)]
        return jnp.stack(p)

    a_tokens = tokens_of([own, up[1], up[2], down[1]], 1)
    a_tokens, up[3] = together(a_tokens, up[3])
    up.append(from_z(up[3], 1))
    a = partials(a_tokens)
    a, up[4] = together(a, up[4])
    a = a.reshape(3, X, YH * block, f)
    b_tokens = tokens_of([up[3], up[4], down[3], down[2]], 2)
    b = partials(b_tokens).reshape(3, YH, X * block, f)
    *a_sends, b_send = together(*[a[:, k].astype(BF) for k in range(1, X)], b[:, 1].astype(BF))
    *a_parts, b_part = together(*[from_x(a_sends[k - 1], X - k) for k in range(1, X)], from_yh(b_send))

    a = a[:, 0]
    for part in a_parts:
        a = a + part.astype(F32)
    a = a.reshape(3, YH, block, f)
    b = (b[:, 0] + b_part.astype(F32)).reshape(3, X, block, f)
    *b_sends, a_send = together(*[b[:, k].astype(BF) for k in range(1, X)], a[:, 1].astype(BF))
    *b_parts, a_part = together(*[from_x(b_sends[k - 1], X - k) for k in range(1, X)], from_yh(a_send))

    a_rows = swiglu_back(*(a[:, 0] + a_part.astype(F32)))
    b = b[:, 0]
    for part in b_parts:
        b = b + part.astype(F32)
    a_rows, b_rows = together(a_rows, swiglu_back(*b))
    *b_parts, a_part = together(*[from_x(b_rows, k) for k in range(1, X)], from_yh(a_rows))

    a_half = jnp.stack([a_rows, a_part], 1).reshape(3, YH * block, f)
    b_half = jnp.stack([b_rows] + b_parts, 1).reshape(3, X * block, f)
    a_half, b_half = together(a_half, b_half)
    *a_parts, b_part = together(*[from_x(a_half, k) for k in range(1, X)], from_yh(b_half))
    order = (x + jnp.arange(X)) % X
    place = jnp.concatenate([(z + (order + 1) % X - 1) % Z, (z + 3 + order) % Z, yh[None]]).astype(jnp.int32)
    early = [dot_last(r[0], gate_weight) + dot_last(r[1], up_weight) for r in (a_half, b_half)]
    blocks = a_parts + [b_part]
    mine, mine_yl, other, other_yl = input_terms(place, blocks, *early, gate_weight, up_weight, t)
    row_blocks = [a_half] + a_parts + [b_half, b_part]
    other_yl = (mine_yl + from_core(other_yl)).astype(BF)
    other, *row_blocks, _ = together(other, *row_blocks, other_yl)
    rows = [jnp.concatenate([r[i] for r in row_blocks]) for i in range(3)]
    tokens_all, grads_all = (jnp.concatenate([a_tokens[i], b_tokens[i]]) for i in (0, 1))
    terms = mine + from_core(other)
    terms, part, *rows = together(terms, from_yl(other_yl), *rows)
    terms = terms + part.astype(F32)
    groups = [[(yl * Z + i) * CORE + c for i in range(Z)] for yl in range(YL) for c in range(CORE)]
    parts = lax.all_to_all(terms.astype(BF), "col", 0, 0, axis_index_groups=groups, tiled=True)
    parts = jnp.where((jnp.arange(Z) == z)[:, None, None], 0.0, parts.astype(F32))
    input_grad = lax.dynamic_index_in_dim(terms, z, 0, keepdims=False) + parts.sum(0)

    grad_gate, grad_up, hidden = rows
    gate_grad = dot_first(tokens_all, grad_gate)
    up_grad = dot_first(tokens_all, grad_up)
    down_grad = dot_first(hidden, grads_all)
    return (input_grad.astype(BF), gate_grad.astype(BF), up_grad.astype(BF), down_grad.astype(BF))


def solution(mesh):
    in_specs = (P("col", "row"), P("col", "row"), P("row", "col"), P("row", "col"), P("col", "row"))
    out_specs = (P("col", "row"), P("row", "col"), P("row", "col"), P("col", "row"))
    return jax.shard_map(
        on_device, mesh=mesh, in_specs=in_specs, out_specs=out_specs, check_vma=False
    )
```

```python
import jax
import jax.numpy as jnp
from jax import lax
from jax.experimental import pallas as pl
from jax.experimental.pallas import tpu as pltpu
from jax.sharding import PartitionSpec as P

BF, F32 = jnp.bfloat16, jnp.float32
YH, X, YL, Z, CORE = 2, 4, 2, 8, 2
LAST = (((1,), (1,)), ((), ()))
FIRST = (((0,), (0,)), ((), ()))


def from_x(block, k):
    blocks = [(h * X + (x + k) % X, h * X + x) for h in range(YH) for x in range(X)]
    return lax.ppermute(block, "row", blocks)


def from_yh(block):
    return lax.ppermute(block, "row", [(i, (i + X) % (X * YH)) for i in range(X * YH)])


def from_col(block, source):
    blocks = []
    for yl in range(YL):
        for z in range(Z):
            for core in range(CORE):
                a, b, c = source(yl, z, core)
                blocks.append(((a * Z + b % Z) * CORE + c, (yl * Z + z) * CORE + core))
    return lax.ppermute(block, "col", blocks)


def from_z(block, k):
    return from_col(block, lambda yl, z, core: (yl, z + k, core))


def from_yl(block):
    return from_col(block, lambda yl, z, core: (1 - yl, z, core))


def from_core(block):
    return from_col(block, lambda yl, z, core: (yl, z, 1 - core))


def dot(a, b):
    return jnp.dot(a, b, preferred_element_type=F32)


def dot_last(a, b):
    return lax.dot_general(a, b, LAST, preferred_element_type=F32)


def dot_first(a, b):
    return lax.dot_general(a, b, FIRST, preferred_element_type=F32)


def together(*blocks):
    return lax.optimization_barrier(blocks)


def swiglu_back(gate, up, grad_hidden):
    sigmoid_gate = jax.nn.sigmoid(gate)
    act = gate * sigmoid_gate
    hidden = (act * up).astype(BF)
    grad_gate = (grad_hidden * up * sigmoid_gate * (1.0 + gate * (1.0 - sigmoid_gate))).astype(BF)
    grad_up = (grad_hidden * act).astype(BF)
    return jnp.stack([grad_gate, grad_up, hidden])


def input_terms_kernel(place, *refs):
    *row_refs, gate_ref, up_ref, mine_ref, mine_yl_ref, other_ref, other_yl_ref, rows = refs

    f = gate_ref.shape[1]

    @pl.when(pl.program_id(0) == 0)
    def _():
        start = 0
        for ref in row_refs:
            rows[start : start + ref.shape[1], :f] = ref[0]
            rows[start : start + ref.shape[1], f:] = ref[1]
            start += ref.shape[1]

    terms = dot_last(rows[...], jnp.concatenate([gate_ref[...], up_ref[...]], 1))
    t = mine_ref.shape[1]
    n = YL * t
    first = place[2 * X] == 0

    def put(at, zero, one):
        zero, one = terms[zero * n : (zero + 1) * n], terms[one * n : (one + 1) * n]
        mine, other = jnp.where(first, zero, one), jnp.where(first, one, zero)
        mine_ref[at], mine_yl_ref[at] = mine[:t], mine[t:]
        other_ref[at], other_yl_ref[at] = other[:t], other[t:]

    for k in range(X):
        put(place[k], YH * k, YH * k + 1)
        put(place[X + k], YH * X + k, YH * X + X + k)


def input_terms(place, row_blocks, gate_weight, up_weight, t):
    f, d = row_blocks[0].shape[2], gate_weight.shape[0]
    total = sum(r.shape[1] for r in row_blocks)
    wide = min(d, 512)
    whole = [pl.BlockSpec((2, r.shape[1], f), lambda i, _: (0, 0, 0)) for r in row_blocks]
    weight = pl.BlockSpec((wide, f), lambda i, _: (i, 0))
    out = pl.BlockSpec((Z, t, wide), lambda i, _: (0, 0, i))
    return pl.pallas_call(
        input_terms_kernel,
        grid_spec=pltpu.PrefetchScalarGridSpec(
            num_scalar_prefetch=1,
            grid=(d // wide,),
            in_specs=whole + [weight, weight],
            out_specs=[out] * 4,
            scratch_shapes=[pltpu.VMEM((total, 2 * f), BF)],
        ),
        out_shape=[jax.ShapeDtypeStruct((Z, t, d), F32)] * 4,
        cost_estimate=pl.CostEstimate(
            flops=4 * total * f * d, bytes_accessed=4 * total * (f + d) + 4 * d * f, transcendentals=0
        ),
        compiler_params=pltpu.CompilerParams(vmem_limit_bytes=60 << 20),
    )(place, *row_blocks, gate_weight, up_weight)


def on_device(inputs, grad_out, gate_weight, up_weight, down_weight):
    row, col = lax.axis_index("row"), lax.axis_index("col")
    yh, x, z = row // X, row % X, col // CORE % Z
    t, d = inputs.shape
    f = gate_weight.shape[1]
    block = YL * t

    own = jnp.stack([inputs, grad_out])
    own = jnp.concatenate([own, from_yl(own)], 1)
    up, down = [own], [own]
    for _ in range(Z // 2 - 1):
        up.append(from_z(up[-1], 1))
        down.append(from_z(down[-1], Z - 1))

    def tokens_of(blocks, axis):
        blocks = [(b, from_core(b)) for b in blocks]
        blocks = [(jnp.where(yh == 0, *b), jnp.where(yh == 0, *b[::-1])) for b in blocks]

        def in_order(blocks):
            tokens = lax.dynamic_slice_in_dim(jnp.stack(blocks + blocks, 1), x, X, 1)
            return tokens.reshape(2, -1, d)

        if axis == 1:
            return in_order([jnp.concatenate(b, 1) for b in blocks])
        return jnp.concatenate([in_order([b[h] for b in blocks]) for h in range(YH)], 1)

    def partials(both):
        p = [dot(both[0], gate_weight), dot(both[0], up_weight), dot_last(both[1], down_weight)]
        return jnp.stack(p)

    a_tokens = tokens_of([own, up[1], up[2], down[1]], 1)
    a_tokens, up[3] = together(a_tokens, up[3])
    up.append(from_z(up[3], 1))
    a = partials(a_tokens)
    a, up[4] = together(a, up[4])
    a = a.reshape(3, X, YH * block, f)
    b_tokens = tokens_of([up[3], up[4], down[3], down[2]], 2)
    b = partials(b_tokens).reshape(3, YH, X * block, f)
    *a_sends, b_send = together(*[a[:, k].astype(BF) for k in range(1, X)], b[:, 1].astype(BF))
    *a_parts, b_part = together(*[from_x(a_sends[k - 1], X - k) for k in range(1, X)], from_yh(b_send))

    a = a[:, 0]
    for part in a_parts:
        a = a + part.astype(F32)
    a = a.reshape(3, YH, block, f)
    b = (b[:, 0] + b_part.astype(F32)).reshape(3, X, block, f)
    *b_sends, a_send = together(*[b[:, k].astype(BF) for k in range(1, X)], a[:, 1].astype(BF))
    *b_parts, a_part = together(*[from_x(b_sends[k - 1], X - k) for k in range(1, X)], from_yh(a_send))

    a_rows = swiglu_back(*(a[:, 0] + a_part.astype(F32)))
    b = b[:, 0]
    for part in b_parts:
        b = b + part.astype(F32)
    a_rows, b_rows = together(a_rows, swiglu_back(*b))
    *b_parts, a_part = together(*[from_x(b_rows, k) for k in range(1, X)], from_yh(a_rows))

    a_half = jnp.stack([a_rows, a_part], 1).reshape(3, YH * block, f)
    b_half = jnp.stack([b_rows] + b_parts, 1).reshape(3, X * block, f)
    a_half, b_half = together(a_half, b_half)
    a_one, a_three = from_x(a_half, 1), from_x(a_half, X - 1)
    a_two = [from_x(a_one[:, :block], 1), from_x(a_three[:, block:], X - 1)]
    *a_parts, b_part = together(a_one, *a_two, a_three, from_yh(b_half))
    order = (x + jnp.arange(X)) % X
    place = jnp.concatenate([(z + (order + 1) % X - 1) % Z, (z + 3 + order) % Z, yh[None]]).astype(jnp.int32)
    row_blocks = [a_half] + a_parts + [b_half, b_part]
    mine, mine_yl, other, other_yl = input_terms(place, row_blocks, gate_weight, up_weight, t)
    other_yl = (mine_yl + from_core(other_yl)).astype(BF)
    other, *row_blocks, _ = together(other, *row_blocks, other_yl)
    rows = [jnp.concatenate([r[i] for r in row_blocks]) for i in range(3)]
    tokens_all, grads_all = (jnp.concatenate([a_tokens[i], b_tokens[i]]) for i in (0, 1))
    terms = mine + from_core(other)
    terms, part, *rows = together(terms, from_yl(other_yl), *rows)
    terms = terms + part.astype(F32)
    groups = [[(yl * Z + i) * CORE + c for i in range(Z)] for yl in range(YL) for c in range(CORE)]
    parts = lax.all_to_all(terms.astype(BF), "col", 0, 0, axis_index_groups=groups, tiled=True)
    parts = jnp.where((jnp.arange(Z) == z)[:, None, None], 0.0, parts.astype(F32))
    input_grad = lax.dynamic_index_in_dim(terms, z, 0, keepdims=False) + parts.sum(0)

    grad_gate, grad_up, hidden = rows
    gate_grad = dot_first(tokens_all, grad_gate)
    up_grad = dot_first(tokens_all, grad_up)
    down_grad = dot_first(hidden, grads_all)
    return (input_grad.astype(BF), gate_grad.astype(BF), up_grad.astype(BF), down_grad.astype(BF))


def solution(mesh):
    in_specs = (P("col", "row"), P("col", "row"), P("row", "col"), P("row", "col"), P("col", "row"))
    out_specs = (P("col", "row"), P("row", "col"), P("row", "col"), P("col", "row"))
    return jax.shard_map(
        on_device, mesh=mesh, in_specs=in_specs, out_specs=out_specs, check_vma=False
    )
```

```python
import jax
import jax.numpy as jnp
from jax import lax
from jax.experimental import pallas as pl
from jax.experimental.pallas import tpu as pltpu
from jax.sharding import PartitionSpec as P

BF, F32 = jnp.bfloat16, jnp.float32
YH, X, YL, Z, CORE = 2, 4, 2, 8, 2
LAST = (((1,), (1,)), ((), ()))
FIRST = (((0,), (0,)), ((), ()))


def from_x(block, k):
    blocks = [(h * X + (x + k) % X, h * X + x) for h in range(YH) for x in range(X)]
    return lax.ppermute(block, "row", blocks)


def from_yh(block):
    return lax.ppermute(block, "row", [(i, (i + X) % (X * YH)) for i in range(X * YH)])


def from_col(block, source):
    blocks = []
    for yl in range(YL):
        for z in range(Z):
            for core in range(CORE):
                a, b, c = source(yl, z, core)
                blocks.append(((a * Z + b % Z) * CORE + c, (yl * Z + z) * CORE + core))
    return lax.ppermute(block, "col", blocks)


def from_z(block, k):
    return from_col(block, lambda yl, z, core: (yl, z + k, core))


def from_yl(block):
    return from_col(block, lambda yl, z, core: (1 - yl, z, core))


def from_core(block):
    return from_col(block, lambda yl, z, core: (yl, z, 1 - core))


def dot(a, b):
    return jnp.dot(a, b, preferred_element_type=F32)


def dot_last(a, b):
    return lax.dot_general(a, b, LAST, preferred_element_type=F32)


def dot_first(a, b):
    return lax.dot_general(a, b, FIRST, preferred_element_type=F32)


def together(*blocks):
    return lax.optimization_barrier(blocks)


def swiglu_back(gate, up, grad_hidden):
    sigmoid_gate = jax.nn.sigmoid(gate)
    act = gate * sigmoid_gate
    hidden = (act * up).astype(BF)
    grad_gate = (grad_hidden * up * sigmoid_gate * (1.0 + gate * (1.0 - sigmoid_gate))).astype(BF)
    grad_up = (grad_hidden * act).astype(BF)
    return jnp.stack([grad_gate, grad_up, hidden])


def input_terms_kernel(place, *refs):
    *row_refs, gate_ref, up_ref, mine_ref, mine_yl_ref, other_ref, other_yl_ref, rows = refs

    f = gate_ref.shape[1]

    @pl.when(pl.program_id(0) == 0)
    def _():
        start = 0
        for ref in row_refs:
            rows[start : start + ref.shape[1], :f] = ref[0]
            rows[start : start + ref.shape[1], f:] = ref[1]
            start += ref.shape[1]

    terms = dot_last(rows[...], jnp.concatenate([gate_ref[...], up_ref[...]], 1))
    t = mine_ref.shape[1]
    n = YL * t
    first = place[2 * X] == 0

    def put(at, zero, one):
        zero, one = terms[zero * n : (zero + 1) * n], terms[one * n : (one + 1) * n]
        mine, other = jnp.where(first, zero, one), jnp.where(first, one, zero)
        mine_ref[at], mine_yl_ref[at] = mine[:t], mine[t:]
        other_ref[at], other_yl_ref[at] = other[:t], other[t:]

    for k in range(X):
        put(place[k], YH * k, YH * k + 1)
        put(place[X + k], YH * X + k, YH * X + X + k)


def input_terms(place, row_blocks, gate_weight, up_weight, t):
    f, d = row_blocks[0].shape[2], gate_weight.shape[0]
    total = sum(r.shape[1] for r in row_blocks)
    wide = min(d, 512)
    whole = [pl.BlockSpec((2, r.shape[1], f), lambda i, _: (0, 0, 0)) for r in row_blocks]
    weight = pl.BlockSpec((wide, f), lambda i, _: (i, 0))
    out = pl.BlockSpec((Z, t, wide), lambda i, _: (0, 0, i))
    return pl.pallas_call(
        input_terms_kernel,
        grid_spec=pltpu.PrefetchScalarGridSpec(
            num_scalar_prefetch=1,
            grid=(d // wide,),
            in_specs=whole + [weight, weight],
            out_specs=[out] * 4,
            scratch_shapes=[pltpu.VMEM((total, 2 * f), BF)],
        ),
        out_shape=[jax.ShapeDtypeStruct((Z, t, d), F32)] * 4,
        cost_estimate=pl.CostEstimate(
            flops=4 * total * f * d, bytes_accessed=4 * total * (f + d) + 4 * d * f, transcendentals=0
        ),
        compiler_params=pltpu.CompilerParams(vmem_limit_bytes=60 << 20),
    )(place, *row_blocks, gate_weight, up_weight)


def on_device(inputs, grad_out, gate_weight, up_weight, down_weight):
    row, col = lax.axis_index("row"), lax.axis_index("col")
    yh, x, z = row // X, row % X, col // CORE % Z
    t, d = inputs.shape
    f = gate_weight.shape[1]
    block = YL * t

    own = jnp.stack([inputs, grad_out])
    own = jnp.concatenate([own, from_yl(own)], 1)
    up, down = [own], [own]
    for _ in range(Z // 2 - 1):
        up.append(from_z(up[-1], 1))
        down.append(from_z(down[-1], Z - 1))

    def tokens_of(blocks, axis):
        blocks = [(b, from_core(b)) for b in blocks]
        blocks = [(jnp.where(yh == 0, *b), jnp.where(yh == 0, *b[::-1])) for b in blocks]

        def in_order(blocks):
            tokens = lax.dynamic_slice_in_dim(jnp.stack(blocks + blocks, 1), x, X, 1)
            return tokens.reshape(2, -1, d)

        if axis == 1:
            return in_order([jnp.concatenate(b, 1) for b in blocks])
        return jnp.concatenate([in_order([b[h] for b in blocks]) for h in range(YH)], 1)

    def partials(both):
        p = [dot(both[0], gate_weight), dot(both[0], up_weight), dot_last(both[1], down_weight)]
        return jnp.stack(p)

    a_tokens = tokens_of([own, up[1], up[2], down[1]], 1)
    a_tokens, up[3] = together(a_tokens, up[3])
    up.append(from_z(up[3], 1))
    a = partials(a_tokens)
    a, up[4] = together(a, up[4])
    a = a.reshape(3, X, YH * block, f)
    b_tokens = tokens_of([up[3], up[4], down[3], down[2]], 2)
    b = partials(b_tokens).reshape(3, YH, X * block, f)
    half = X // 2 * block
    halves = [b[:, 1, :half].astype(BF), b[:, 1, half:].astype(BF)]
    *a_sends, low, high = together(*[a[:, k].astype(BF) for k in range(1, X)], *halves)
    parts = [from_x(a_sends[k - 1], X - k) for k in range(1, X)]
    *a_parts, low, high = together(*parts, from_yh(low), from_yh(high))

    a = a[:, 0]
    for part in a_parts:
        a = a + part.astype(F32)
    a = a.reshape(3, YH, block, f)
    b = b[:, 0].reshape(3, X, block, f)
    b_part = [p.reshape(3, X // 2, block, f)[:, k] for p in (low, high) for k in range(X // 2)]
    b = [b[:, k] + b_part[k].astype(F32) for k in range(X)]
    *b_sends, a_send = together(*[b[k].astype(BF) for k in range(1, X)], a[:, 1].astype(BF))
    *b_parts, a_part = together(*[from_x(b_sends[k - 1], X - k) for k in range(1, X)], from_yh(a_send))

    a_rows = swiglu_back(*(a[:, 0] + a_part.astype(F32)))
    b = b[0]
    for part in b_parts:
        b = b + part.astype(F32)
    a_rows, b_rows = together(a_rows, swiglu_back(*b))
    *b_parts, a_part = together(*[from_x(b_rows, k) for k in range(1, X)], from_yh(a_rows))

    a_half = jnp.stack([a_rows, a_part], 1).reshape(3, YH * block, f)
    b_half = jnp.stack([b_rows] + b_parts, 1).reshape(3, X * block, f)
    a_half, b_half = together(a_half, b_half)
    a_one, a_three = from_x(a_half, 1), from_x(a_half, X - 1)
    a_two = [from_x(a_one[:, :block], 1), from_x(a_three[:, block:], X - 1)]
    *a_parts, b_part = together(a_one, *a_two, a_three, from_yh(b_half))
    order = (x + jnp.arange(X)) % X
    place = jnp.concatenate([(z + (order + 1) % X - 1) % Z, (z + 3 + order) % Z, yh[None]]).astype(jnp.int32)
    row_blocks = [a_half] + a_parts + [b_half, b_part]
    mine, mine_yl, other, other_yl = input_terms(place, row_blocks, gate_weight, up_weight, t)
    other_yl = (mine_yl + from_core(other_yl)).astype(BF)
    other, *row_blocks, _ = together(other, *row_blocks, other_yl)
    rows = [jnp.concatenate([r[i] for r in row_blocks]) for i in range(3)]
    tokens_all, grads_all = (jnp.concatenate([a_tokens[i], b_tokens[i]]) for i in (0, 1))
    terms = mine + from_core(other)
    terms, part, *rows = together(terms, from_yl(other_yl), *rows)
    terms = terms + part.astype(F32)
    groups = [[(yl * Z + i) * CORE + c for i in range(Z)] for yl in range(YL) for c in range(CORE)]
    parts = lax.all_to_all(terms.astype(BF), "col", 0, 0, axis_index_groups=groups, tiled=True)
    parts = jnp.where((jnp.arange(Z) == z)[:, None, None], 0.0, parts.astype(F32))
    input_grad = lax.dynamic_index_in_dim(terms, z, 0, keepdims=False) + parts.sum(0)

    grad_gate, grad_up, hidden = rows
    gate_grad = dot_first(tokens_all, grad_gate)
    up_grad = dot_first(tokens_all, grad_up)
    down_grad = dot_first(hidden, grads_all)
    return (input_grad.astype(BF), gate_grad.astype(BF), up_grad.astype(BF), down_grad.astype(BF))


def solution(mesh):
    in_specs = (P("col", "row"), P("col", "row"), P("row", "col"), P("row", "col"), P("col", "row"))
    out_specs = (P("col", "row"), P("row", "col"), P("row", "col"), P("col", "row"))
    return jax.shard_map(
        on_device, mesh=mesh, in_specs=in_specs, out_specs=out_specs, check_vma=False
    )
```
